256 devices in a mesh: blk: 8 (over y_lo, x), grp: 32 (over z, y_hi, core).
Axes of the slice: x: 4, y: 4 (y_hi: 2, y_lo: 2; y = y_hi * 2 + y_lo), z: 8, core: 2. Of those that a mesh axis runs over, the one named last changes fastest.
Arguments:
- gate_pre: bfloat16 [4096, 2, 8192], P('blk', None, 'grp'), may hold values from -6 to 6
- up_pre: bfloat16 [4096, 2, 8192], P('blk', None, 'grp'), may hold values from -6 to 6
- first_share: float32 [4096], P('blk'), may hold values from 0.1 to 0.9
- expert_ids: int32 [4096, 2], P('blk'), may hold values from 0 to 7, all different within a row; in each aligned block of 512 rows (0 to 511, 512 to 1023, ...) at most 256 rows name the same one
- down_weight: bfloat16 [8, 8192, 6144], P('blk', 'grp'), may hold values from -0.0625 to 0.0625
Outputs:
- mixed: bfloat16 [4096, 6144], P(('blk', 'grp'))
The draws below stay inside these ranges and needn't reach their ends.
Inputs may be any that keep to these rules, and one draw needn't show every extreme that they name: `expert_ids`: the 2 ids of a token differ. In each group's aligned block of 512 tokens no expert is named by more than 256 ids, a bound that some block reaches.
All inputs are finite; a program needn't handle non-finite values.
Results may differ from the reference program's by a relative error of at most 0.02.
Values may be sent and summed in bfloat16 or wider, within the bound.
No kernel may reach another device: no remote copies, remote signals or barrier semaphores. Data moves between devices by JAX's collectives and lax.ppermute only.
A program may use at most 192 MiB of HBM per device.

```python
import math
import jax
import jax.numpy as jnp
import numpy as np
from jax import lax

D = 6144
FF_DEV = 256
TOP = 2
TOK_GRP = 512
E = 8
FF = 8192
CAP = 256
TOKENS = 4096
N_BLK = 8
N_GRP = 32


def with_spikes(entries, stream_key, source, target, shards_of, factor):
    owner, partner = [(jnp.arange(entries.shape[position]) // (entries.shape[position] // shards_of)).reshape([-1 if axis == position else 1 for axis in range(entries.ndim)]) for position in (source, target)]
    chosen = jax.random.permutation(stream_key, shards_of)[partner]
    strong = (owner == chosen) | (owner == (partner + shards_of // 2) % shards_of)
    return jnp.where(strong, factor * entries, entries)


def block_scale(key, shape, shards, least, top_value):
    gain = 1.0
    for axis_at, blocks in shards:
        heights = jax.random.uniform(jax.random.fold_in(jax.random.fold_in(key, 6), axis_at), (blocks,), jnp.float32, least / len(shards), top_value / len(shards))
        gain = gain * jnp.repeat(jnp.exp(heights), shape[axis_at] // blocks).reshape((-1,) + (1,) * (len(shape) - 1 - axis_at))
    return gain


def shared_out(stream_key, own, number, rows, number_of, top, limit, skew):
    order = jax.random.permutation(stream_key, number_of)
    packed, common = portions_of(number_of, rows * top, limit, skew, True), portions_of(number_of, rows * top, limit, skew, False)
    places = jnp.arange(number_of)

    def named(sizes, offset_by):
        used = int((sizes > 0).sum())
        fixed = max(1, used // 4)
        shifted = fixed + (places - fixed + offset_by * (used - fixed)) % max(1, number_of - fixed)
        return jnp.zeros((number_of,), jnp.int32).at[order[jnp.where(places < fixed, places, shifted)]].set(jnp.asarray(sizes, jnp.int32))

    sizes = jnp.where(number % 4 == 0, named(packed, number // 4), named(common, number - number // 4 - 1))
    mixed = jax.random.permutation(jax.random.fold_in(own, 3), number_of)
    source_of, sink = mixed[0:number_of // 2 * 2:2], mixed[1:number_of // 2 * 2:2]
    margin = jnp.minimum(sizes[source_of] - 1, limit - sizes[sink]) // 2
    margin = jnp.where((source_of == order[0]) | (sink == order[0]) | (sizes[sink] == 0), 0, jnp.maximum(margin, 0))
    shifted = jax.random.randint(jax.random.fold_in(own, 4), (number_of // 2,), 0, 1 << 20) % (margin + 1)
    sizes = sizes.at[source_of].add(-shifted).at[sink].add(shifted)
    labels = jnp.searchsorted(jnp.cumsum(sizes), jnp.arange(rows * top), side="right").astype(jnp.int32)
    grid = labels.reshape(top, rows).T
    grid = grid[jax.random.permutation(jax.random.fold_in(own, 1), rows)]
    offset_by = jax.random.randint(jax.random.fold_in(own, 2), (rows, 1), 0, top)
    return jnp.take_along_axis(grid, (jnp.arange(top)[None, :] + offset_by) % top, axis=1)


def portions_of(amount, total, limit, lean, full):
    loads = [(1 << 20) // math.isqrt(grade ** lean) + 1 for grade in range(1, amount + 1)]
    largest = limit if full else min(limit, max(-(-total // amount), total * loads[0] // sum(loads)))
    least = 1 if total - largest >= amount - 1 else 0
    given, spare = [largest] + [least] * (amount - 1), total - largest - least * (amount - 1)
    while spare > 0:
        free = [i for i in range(1, amount) if given[i] < largest] or [i for i in range(1, amount) if given[i] < limit]
        mass, left = sum([loads[i] for i in free]), spare
        for i in free:
            extra = min(limit - given[i], max(1, left * loads[i] // mass), spare)
            given[i] = given[i] + extra
            spare = spare - extra
    return np.array(given)


def centred(key, dims, width, reach, cuts=(), kind=jnp.bfloat16):
    level = block_scale(key, dims, cuts, -0.22, 0.18) if cuts else 1.0
    drawn = jax.random.normal(key, dims, jnp.float32) * width * level
    return jnp.minimum(jnp.maximum(drawn, -reach), reach).astype(kind)


def heavy_noise(own_key, shape, scale, most, shards, heavy, kind=jnp.bfloat16):
    entries = scale * jax.random.normal(own_key, shape, jnp.float32)
    if shards:
        entries = entries * block_scale(own_key, shape, shards, -0.22, 0.18)
    return jnp.clip(with_spikes(entries, jax.random.fold_in(own_key, 3), *heavy), -most, most).astype(kind)


def setup_inputs(seed: int = 0) -> dict:
    keys = jax.random.split(jax.random.key(seed), 6)
    gate_pre = centred(keys[0], (TOKENS, TOP, FF), 1.0, 6.0, ((0, 8), (2, 32)))
    up_pre = heavy_noise(keys[1], (TOKENS, TOP, FF), 1.0, 6.0, ((0, 8), (2, 32)), (2, 0, 32, 2.75))
    first_share = jnp.clip(0.1 + 0.79999997 * jax.random.uniform(keys[2], (TOKENS,), jnp.float32) ** block_scale(keys[2], (TOKENS,), ((0, 8),), -0.2, 0.2), 0.1, 0.9)
    expert_ids_keys = jax.random.split(jax.random.fold_in(keys[3], 1), TOKENS // TOK_GRP)
    expert_ids_turns = jax.random.permutation(jax.random.fold_in(keys[3], 3), TOKENS // TOK_GRP)
    expert_ids = jax.vmap(lambda own, number: shared_out(jax.random.fold_in(keys[3], 2), own, number, TOK_GRP, E, TOP, CAP, 2))(expert_ids_keys, expert_ids_turns).reshape((TOKENS, TOP))
    down_weight = centred(keys[4], (E, FF, D), FF ** -0.5, 0.0625, ((0, 8), (1, 32)))
    return {"gate_pre": gate_pre, "up_pre": up_pre, "first_share": first_share, "expert_ids": expert_ids, "down_weight": down_weight}


def build_table(group_ids, experts, capacity):
    flat_ids = group_ids.reshape(-1).astype(jnp.int32)
    row_total = flat_ids.shape[0]
    onehot = (flat_ids[:, None] == jnp.arange(experts, dtype=jnp.int32)[None, :]).astype(jnp.int32)
    rank_rows = jnp.cumsum(onehot, axis=0) - 1
    slot_of = jnp.sum(rank_rows * onehot, axis=1).astype(jnp.int32)
    slot_table = jnp.full((experts, capacity), row_total, jnp.int32)
    slot_table = slot_table.at[flat_ids, slot_of].set(jnp.arange(row_total, dtype=jnp.int32))
    return slot_table


def reference(gate_pre, up_pre, first_share, expert_ids, down_weight):
    slot_weight = jnp.stack([first_share, 1.0 - first_share], axis=1).astype(jnp.float32)
    hidden = (slot_weight[:, :, None] * jax.nn.silu(gate_pre.astype(jnp.float32)) * up_pre.astype(jnp.float32)).astype(jnp.bfloat16)
    hidden = hidden.reshape(N_BLK, TOK_GRP, TOP, FF)
    group_ids = expert_ids.reshape(N_BLK, TOK_GRP, TOP)

    def one_group(operands):
        group_hidden, ids_here = operands
        rows_flat = group_hidden.reshape(TOK_GRP * TOP, FF)
        padded = jnp.concatenate([rows_flat, jnp.zeros((1, FF), jnp.bfloat16)], axis=0)
        slot_table = build_table(ids_here, E, CAP)

        def one_expert(partial_value, expert):
            row_ids = slot_table[expert]
            picked = padded[row_ids].astype(jnp.float32).reshape(CAP, N_GRP, FF_DEV)
            weight = down_weight[expert].astype(jnp.float32).reshape(N_GRP, FF_DEV, D)
            product = jnp.einsum("cjf,jfd->jcd", picked, weight)
            return partial_value.at[:, row_ids // 2].add(product, mode="drop"), None

        start = jnp.zeros((N_GRP, TOK_GRP, D), jnp.float32)
        partial_value, ignored = lax.scan(one_expert, start, jnp.arange(E, dtype=jnp.int32))
        rounded = lax.optimization_barrier(partial_value.astype(jnp.bfloat16)).astype(jnp.float32)
        return jnp.sum(rounded, axis=0).astype(jnp.bfloat16)

    mixed = lax.map(one_group, (hidden, group_ids))
    return mixed.reshape(TOKENS, D)
```

```python
import jax
import jax.numpy as jnp
from jax import lax
from jax.experimental import pallas as pl
from jax.experimental.pallas import tpu as pltpu
from jax.sharding import PartitionSpec as P

N_CORE = 2
N_YHI = 2


def mix_kernel(ids_ref, hidden_ref, weight_ref, out_ref, wide_ref):
    experts = weight_ref.shape[0]
    units = weight_ref.shape[1]
    ids = ids_ref[0]
    first, second = hidden_ref[0, :, :units], hidden_ref[0, :, units:]
    for expert in range(experts):
        chosen = (ids == expert).astype(jnp.float32).astype(jnp.bfloat16)
        wide_ref[:, expert * units : (expert + 1) * units] = (
            first * chosen[:, 0:1] + second * chosen[:, 1:2]
        )
    weight = weight_ref[...].reshape(experts * units, weight_ref.shape[2])
    total = jnp.dot(wide_ref[...], weight, preferred_element_type=jnp.float32)
    out_ref[...] = total.astype(jnp.bfloat16).reshape(out_ref.shape)


def mix(ids, hidden, weight, out_dims):
    groups, rows, width = hidden.shape
    experts, units, columns = weight.shape
    cores, depth, keep = out_dims
    return pl.pallas_call(
        mix_kernel,
        grid=(groups,),
        in_specs=[
            pl.BlockSpec((1, rows, 2), lambda g: (g, 0, 0)),
            pl.BlockSpec((1, rows, width), lambda g: (g, 0, 0)),
            pl.BlockSpec((experts, units, columns), lambda g: (0, 0, 0)),
        ],
        out_specs=pl.BlockSpec((cores, depth, 1, keep, columns), lambda g: (0, 0, g, 0, 0)),
        out_shape=jax.ShapeDtypeStruct((cores, depth, groups, keep, columns), jnp.bfloat16),
        scratch_shapes=[pltpu.VMEM((rows, experts * units), jnp.bfloat16)],
        compiler_params=pltpu.CompilerParams(vmem_limit_bytes=48 * 1024 * 1024),
        cost_estimate=pl.CostEstimate(
            flops=2 * groups * rows * experts * units * columns,
            bytes_accessed=2 * (groups * rows * (width + columns) + experts * units * columns),
            transcendentals=0,
        ),
    )(ids, hidden, weight)


def on_device(gate_pre, up_pre, first_share, expert_ids, down_weight):
    n_blk, n_grp = lax.axis_size("blk"), lax.axis_size("grp")
    j = lax.axis_index("grp")
    core, y_hi = j % N_CORE, (j // N_CORE) % N_YHI
    n_z = n_grp // (N_CORE * N_YHI)
    rows, _, units = gate_pre.shape
    keep = rows // n_grp
    columns = down_weight.shape[2] // n_blk
    slot_weight = jnp.stack([first_share, 1.0 - first_share], axis=1)
    hidden = (
        slot_weight[:, :, None]
        * jax.nn.silu(gate_pre.astype(jnp.float32))
        * up_pre.astype(jnp.float32)
    ).astype(jnp.bfloat16)

    def mine_first(x):
        x = x.reshape((n_z * N_YHI, N_CORE, keep) + x.shape[1:])
        mine = lax.dynamic_index_in_dim(x, core, 1, keepdims=False)
        other = lax.dynamic_index_in_dim(x, 1 - core, 1, keepdims=False)
        return jnp.stack([mine, other]).reshape((rows,) + x.shape[3:])

    hidden = mine_first(hidden.reshape(rows, 2 * units))
    ids = mine_first(expert_ids)
    weight = lax.all_to_all(down_weight[0], "blk", 1, 0, tiled=True)
    weight = weight.reshape(n_blk, units, columns)
    hidden_all = lax.all_gather(hidden, "blk")
    ids_all = lax.all_gather(ids, "blk")
    partial = mix(ids_all, hidden_all, weight, (N_CORE, n_z * N_YHI, keep))

    def plus(a, b):
        return (a.astype(jnp.float32) + b.astype(jnp.float32)).astype(jnp.bfloat16)

    other_core = [(i, i ^ 1) for i in range(n_grp)]
    both = plus(partial[0], lax.ppermute(partial[1], "grp", other_core))
    along_z = [[i + z * N_CORE * N_YHI for z in range(n_z)] for i in range(N_CORE * N_YHI)]
    over_z = lax.psum_scatter(
        both, "grp", scatter_dimension=0, axis_index_groups=along_z, tiled=True
    )
    other_y = [(i, i ^ 2) for i in range(n_grp)]
    kept = lax.dynamic_index_in_dim(over_z, y_hi, 0, keepdims=False)
    sent = lax.dynamic_index_in_dim(over_z, 1 - y_hi, 0, keepdims=False)
    summed = plus(kept, lax.ppermute(sent, "grp", other_y))
    pieces = lax.all_to_all(summed, "blk", 0, 0, tiled=True)
    return jnp.swapaxes(pieces, 0, 1).reshape(keep, n_blk * columns)


def solution(mesh):
    in_specs = (
        P("blk", None, "grp"),
        P("blk", None, "grp"),
        P("blk"),
        P("blk", None),
        P("blk", "grp", None),
    )
    out_specs = P(("blk", "grp"), None)
    return jax.shard_map(
        on_device, mesh=mesh, in_specs=in_specs, out_specs=out_specs, check_vma=False
    )
```

```python
import jax
import jax.numpy as jnp
from jax import lax
from jax.experimental import pallas as pl
from jax.experimental.pallas import tpu as pltpu
from jax.sharding import Mesh, PartitionSpec as P

ID_ROWS = 16
LONG = 10**12
LIMIT = 56 * 1024 * 1024
HBM = pl.BlockSpec(memory_space=pl.ANY)
SMEM = pl.BlockSpec(memory_space=pltpu.SMEM)
VMEM = pl.BlockSpec(memory_space=pltpu.VMEM)


def mix_kernel(count, experts, turned, place_ref, *refs):
    messages, weights = refs[:count], refs[count : count + experts]
    mine_ref, other_ref, weight_ref, message_ref, wide_ref, got_weight, got_message = refs[
        count + experts :
    ]
    rows = wide_ref.shape[1]
    units = weight_ref.shape[0] // experts
    depth, keep = mine_ref.shape[0], mine_ref.shape[2]
    columns = weight_ref.shape[1]
    copies = [
        pltpu.make_async_copy(message, message_ref.at[i], got_message.at[i])
        for i, message in enumerate(messages)
    ]
    loads = [
        pltpu.make_async_copy(
            weight, weight_ref.at[pl.ds(e * units, units)], got_weight.at[e]
        )
        for e, weight in enumerate(weights)
    ]
    for load in copies + loads:
        load.start()
    is_odd = place_ref[0] == 1
    for load in copies + loads:
        load.wait()
    for i in range(count):
        ids = jnp.transpose(message_ref[i, rows:, :].astype(jnp.float32))
        first, second = message_ref[i, :rows, :units], message_ref[i, :rows, units:]
        for e in range(experts):
            expert = place_ref[2 + e].astype(jnp.float32)
            chosen = (ids == expert).astype(jnp.float32).astype(jnp.bfloat16)
            wide_ref[i % 2, :, e * units : (e + 1) * units] = (
                first * chosen[:, 0:1] + second * chosen[:, 1:2]
            )
        total = jnp.dot(wide_ref[i % 2], weight_ref[...], preferred_element_type=jnp.float32)
        total = total.astype(jnp.bfloat16).reshape(depth, 2, keep, columns)
        even, odd = total[:, 0], total[:, 1]
        mine, other = jnp.where(is_odd, odd, even), jnp.where(is_odd, even, odd)
        if not turned:
            mine_ref[:, i] = mine
            other_ref[:, i] = other
            continue
        for z in range(depth // 2):
            at = (z - place_ref[1] + depth // 2) % (depth // 2) * 2
            mine_ref[pl.ds(at, 2), i] = mine[2 * z : 2 * z + 2]
            other_ref[pl.ds(at, 2), i] = other[2 * z : 2 * z + 2]


def mix(messages, weights, place, depth, turned):
    count, experts = len(messages), len(weights)
    rows, width = messages[0].shape
    rows -= ID_ROWS
    units, columns = weights[0].shape
    keep = rows // depth // 2
    shape = jax.ShapeDtypeStruct((depth, count, keep, columns), jnp.bfloat16)
    return pl.pallas_call(
        lambda *refs: mix_kernel(count, experts, turned, *refs),
        in_specs=[SMEM] + [HBM] * (count + experts),
        out_specs=[VMEM, VMEM],
        out_shape=[shape, shape],
        scratch_shapes=[
            pltpu.VMEM((experts * units, columns), jnp.bfloat16),
            pltpu.VMEM((count, rows + ID_ROWS, width), jnp.bfloat16),
            pltpu.VMEM((2, rows, experts * units), jnp.bfloat16),
            pltpu.SemaphoreType.DMA((experts,)),
            pltpu.SemaphoreType.DMA((count,)),
        ],
        compiler_params=pltpu.CompilerParams(vmem_limit_bytes=LIMIT),
        cost_estimate=pl.CostEstimate(flops=LONG, bytes_accessed=1000, transcendentals=0),
    )(place, *messages, *weights)


def cut_kernel(order_ref, x_ref, *refs):
    outs, sem = refs[:-1], refs[-1]
    columns = outs[0].shape[1]
    copies = [
        pltpu.make_async_copy(
            x_ref.at[:, pl.ds(pl.multiple_of(order_ref[p] * columns, columns), columns)],
            out,
            sem.at[p],
        )
        for p, out in enumerate(outs)
    ]
    for copy in copies:
        copy.start()
    for copy in copies:
        copy.wait()


def cut(x, order):
    parts = order.shape[0]
    rows, columns = x.shape
    shape = jax.ShapeDtypeStruct((rows, columns // parts), x.dtype)
    return pl.pallas_call(
        cut_kernel,
        in_specs=[SMEM, VMEM],
        out_specs=[HBM] * parts,
        out_shape=[shape] * parts,
        scratch_shapes=[pltpu.SemaphoreType.DMA((parts,))],
        compiler_params=pltpu.CompilerParams(vmem_limit_bytes=LIMIT),
        cost_estimate=pl.CostEstimate(
            flops=0, bytes_accessed=4 * rows * columns, transcendentals=0
        ),
    )(order, x)


def wide_sum(*terms):
    return sum(t.astype(jnp.float32) for t in terms).astype(jnp.bfloat16)


def shift(value, axis, by):
    size = lax.axis_size(axis)
    return lax.ppermute(value, axis, [(i, (i + by) % size) for i in range(size)])


def on_device(gate_pre, up_pre, first_share, expert_ids, down_weight):
    n_x, n_z, n_y = lax.axis_size("x"), lax.axis_size("z"), lax.axis_size("y_hi")
    x, y, z = (lax.axis_index(a).astype(jnp.int32) for a in ("x", "y_lo", "z"))
    core = lax.axis_index("core").astype(jnp.int32)
    rows, _, units = gate_pre.shape
    columns = down_weight.shape[2] // (2 * n_x)
    depth = n_z * n_y
    keep = rows // depth // 2
    slot_weight = jnp.stack([first_share, 1.0 - first_share], axis=1)
    hidden = (
        slot_weight[:, :, None]
        * jax.nn.silu(gate_pre.astype(jnp.float32))
        * up_pre.astype(jnp.float32)
    ).astype(jnp.bfloat16)
    id_rows = jnp.pad(expert_ids.T.astype(jnp.bfloat16), ((0, ID_ROWS - 2), (0, 0)))
    here = jnp.concatenate([hidden.reshape(rows, 2 * units), id_rows], axis=0)

    across = shift(here, "y_lo", 1)
    left, right, far = shift(here, "x", 1), shift(here, "x", -1), shift(here, "x", 2)
    left_across, right_across = shift(across, "x", 1), shift(across, "x", -1)
    far_across = shift(far, "y_lo", 1)

    steps = [(dy, dx) for dx in (0, 2, 1, 3) for dy in (0, 1)]
    to = jnp.stack([(y + dy) % 2 * n_x + (x + dx) % n_x for dy, dx in steps])
    source = [(y + dy) % 2 * n_x + (x - dx) % n_x for dy, dx in steps]
    weights = list(cut(down_weight[0], to))
    for i, (dy, dx) in enumerate(steps):
        if i:
            pairs = [
                (b, (b // n_x + dy) % 2 * n_x + (b + dx) % n_x) for b in range(2 * n_x)
            ]
            weights[i] = lax.ppermute(weights[i], ("y_lo", "x"), pairs)

    place = jnp.stack([core, z] + source)

    def both_cores(messages, turned):
        mine, other = mix(messages, weights, place, depth, turned)
        return mine, lax.ppermute(other, "core", [(0, 1), (1, 0)])

    most = wide_sum(*both_cores([here, across, right, left], False))
    most = lax.psum_scatter(most, "z", scatter_dimension=0, tiled=True)
    rest = both_cores([left_across, right_across, far_across, far], True)

    def terms(by):
        return [r[n_y * by : n_y * (by + 1)] for r in rest]

    half = n_z // 2
    up = wide_sum(*terms(half))
    for by in range(half - 1, 0, -1):
        up = wide_sum(shift(up, "z", 1), *terms(by))
    down = wide_sum(*terms(half + 1))
    for by in range(half + 2, n_z):
        down = wide_sum(shift(down, "z", -1), *terms(by))
    rest = wide_sum(shift(up, "z", 1), shift(down, "z", -1), *terms(0))

    by_place = jnp.stack(
        [
            jnp.stack([most[:, 0], most[:, 2], rest[:, 3], most[:, 3]], axis=1),
            jnp.stack([most[:, 1], rest[:, 1], rest[:, 2], rest[:, 0]], axis=1),
        ],
        axis=1,
    )
    by_place = jnp.where(y == 1, by_place[:, ::-1], by_place)
    by_place = lax.dynamic_slice_in_dim(
        jnp.concatenate([by_place, by_place], axis=2), (n_x - x) % n_x, n_x, axis=2
    )
    pieces = by_place.reshape(n_y * 2 * n_x, keep, columns)
    pieces = lax.all_to_all(pieces, ("y_hi", "y_lo", "x"), 0, 0, tiled=True)
    pieces = pieces.reshape(n_y, 2 * n_x, keep, columns)
    total = wide_sum(pieces[0], pieces[1])
    return jnp.swapaxes(total, 0, 1).reshape(keep, 2 * n_x * columns)


def solution(mesh):
    names = ("y_lo", "x", "z", "y_hi", "core")
    split = Mesh(mesh.devices.reshape(2, mesh.shape["blk"] // 2, mesh.shape["grp"] // 4, 2, 2), names)
    blk, grp = names[:2], names[2:]
    in_specs = (P(blk, None, grp), P(blk, None, grp), P(blk), P(blk, None), P(blk, grp, None))
    return jax.shard_map(
        on_device, mesh=split, in_specs=in_specs, out_specs=P(names, None), check_vma=False
    )
```

```python
import jax
import jax.numpy as jnp
from jax import lax
from jax.experimental import pallas as pl
from jax.experimental.pallas import tpu as pltpu
from jax.sharding import Mesh, PartitionSpec as P

ID_ROWS = 16
LONG = 10**12
LIMIT = 56 * 1024 * 1024
HBM = pl.BlockSpec(memory_space=pl.ANY)
SMEM = pl.BlockSpec(memory_space=pltpu.SMEM)
VMEM = pl.BlockSpec(memory_space=pltpu.VMEM)


def mix_kernel(count, experts, turned, place_ref, *refs):
    messages, weights = refs[:count], refs[count : count + experts]
    mine_ref, other_ref, weight_ref, message_ref, wide_ref, got_weight, got_message = refs[
        count + experts :
    ]
    rows = wide_ref.shape[1]
    units = weight_ref.shape[0] // experts
    depth, keep = mine_ref.shape[0], mine_ref.shape[2]
    columns = weight_ref.shape[1]
    copies = [
        pltpu.make_async_copy(message, message_ref.at[i], got_message.at[i])
        for i, message in enumerate(messages)
    ]
    loads = [
        pltpu.make_async_copy(
            weight, weight_ref.at[pl.ds(e * units, units)], got_weight.at[e]
        )
        for e, weight in enumerate(weights)
    ]
    for load in copies + loads:
        load.start()
    is_odd = place_ref[0] == 1
    for load in copies + loads:
        load.wait()
    for i in range(count):
        ids = jnp.transpose(message_ref[i, rows:, :].astype(jnp.float32))
        first, second = message_ref[i, :rows, :units], message_ref[i, :rows, units:]
        for e in range(experts):
            expert = place_ref[2 + e].astype(jnp.float32)
            chosen = (ids == expert).astype(jnp.float32).astype(jnp.bfloat16)
            wide_ref[i % 2, :, e * units : (e + 1) * units] = (
                first * chosen[:, 0:1] + second * chosen[:, 1:2]
            )
        total = jnp.dot(wide_ref[i % 2], weight_ref[...], preferred_element_type=jnp.float32)
        total = total.astype(jnp.bfloat16).reshape(depth, 2, keep, columns)
        even, odd = total[:, 0], total[:, 1]
        mine, other = jnp.where(is_odd, odd, even), jnp.where(is_odd, even, odd)
        if not turned:
            mine_ref[:, i] = mine
            other_ref[:, i] = other
            continue
        for z in range(depth // 2):
            at = (z - place_ref[1] + depth // 2) % (depth // 2) * 2
            mine_ref[pl.ds(at, 2), i] = mine[2 * z : 2 * z + 2]
            other_ref[pl.ds(at, 2), i] = other[2 * z : 2 * z + 2]


def mix(messages, weights, place, depth, turned):
    count, experts = len(messages), len(weights)
    rows, width = messages[0].shape
    rows -= ID_ROWS
    units, columns = weights[0].shape
    keep = rows // depth // 2
    shape = jax.ShapeDtypeStruct((depth, count, keep, columns), jnp.bfloat16)
    return pl.pallas_call(
        lambda *refs: mix_kernel(count, experts, turned, *refs),
        in_specs=[SMEM] + [HBM] * (count + experts),
        out_specs=[VMEM, VMEM],
        out_shape=[shape, shape],
        scratch_shapes=[
            pltpu.VMEM((experts * units, columns), jnp.bfloat16),
            pltpu.VMEM((count, rows + ID_ROWS, width), jnp.bfloat16),
            pltpu.VMEM((2, rows, experts * units), jnp.bfloat16),
            pltpu.SemaphoreType.DMA((experts,)),
            pltpu.SemaphoreType.DMA((count,)),
        ],
        compiler_params=pltpu.CompilerParams(vmem_limit_bytes=LIMIT),
        cost_estimate=pl.CostEstimate(flops=LONG, bytes_accessed=1000, transcendentals=0),
    )(place, *messages, *weights)


def cut_kernel(order_ref, x_ref, *refs):
    outs, sem = refs[:-1], refs[-1]
    columns = outs[0].shape[1]
    copies = [
        pltpu.make_async_copy(
            x_ref.at[:, pl.ds(pl.multiple_of(order_ref[p] * columns, columns), columns)],
            out,
            sem.at[p],
        )
        for p, out in enumerate(outs)
    ]
    for copy in copies:
        copy.start()
    for copy in copies:
        copy.wait()


def cut(x, order):
    parts = order.shape[0]
    rows, columns = x.shape
    shape = jax.ShapeDtypeStruct((rows, columns // parts), x.dtype)
    return pl.pallas_call(
        cut_kernel,
        in_specs=[SMEM, VMEM],
        out_specs=[VMEM] * parts,
        out_shape=[shape] * parts,
        scratch_shapes=[pltpu.SemaphoreType.DMA((parts,))],
        compiler_params=pltpu.CompilerParams(vmem_limit_bytes=LIMIT),
        cost_estimate=pl.CostEstimate(
            flops=0, bytes_accessed=4 * rows * columns, transcendentals=0
        ),
    )(order, x)


def wide_sum(*terms):
    return sum(t.astype(jnp.float32) for t in terms).astype(jnp.bfloat16)


def shift(value, axis, by):
    size = lax.axis_size(axis)
    return lax.ppermute(value, axis, [(i, (i + by) % size) for i in range(size)])


def on_device(gate_pre, up_pre, first_share, expert_ids, down_weight):
    n_x, n_z, n_y = lax.axis_size("x"), lax.axis_size("z"), lax.axis_size("y_hi")
    x, y, z = (lax.axis_index(a).astype(jnp.int32) for a in ("x", "y_lo", "z"))
    core = lax.axis_index("core").astype(jnp.int32)
    rows, _, units = gate_pre.shape
    columns = down_weight.shape[2] // (2 * n_x)
    depth = n_z * n_y
    keep = rows // depth // 2
    slot_weight = jnp.stack([first_share, 1.0 - first_share], axis=1)
    hidden = (
        slot_weight[:, :, None]
        * jax.nn.silu(gate_pre.astype(jnp.float32))
        * up_pre.astype(jnp.float32)
    ).astype(jnp.bfloat16)
    id_rows = jnp.pad(expert_ids.T.astype(jnp.bfloat16), ((0, ID_ROWS - 2), (0, 0)))
    here = jnp.concatenate([hidden.reshape(rows, 2 * units), id_rows], axis=0)

    across = shift(here, "y_lo", 1)
    left, right, far = shift(here, "x", 1), shift(here, "x", -1), shift(here, "x", 2)
    left_across, right_across = shift(across, "x", 1), shift(across, "x", -1)
    far_across = shift(far, "y_lo", 1)

    steps = [(dy, dx) for dx in (0, 2, 1, 3) for dy in (0, 1)]
    to = jnp.stack([(y + dy) % 2 * n_x + (x + dx) % n_x for dy, dx in steps])
    source = [(y + dy) % 2 * n_x + (x - dx) % n_x for dy, dx in steps]
    weights = list(cut(down_weight[0], to))
    for i, (dy, dx) in enumerate(steps):
        if i:
            pairs = [
                (b, (b // n_x + dy) % 2 * n_x + (b + dx) % n_x) for b in range(2 * n_x)
            ]
            weights[i] = lax.ppermute(weights[i], ("y_lo", "x"), pairs)

    place = jnp.stack([core, z] + source)

    def both_cores(messages, turned):
        mine, other = mix(messages, weights, place, depth, turned)
        return mine, lax.ppermute(other, "core", [(0, 1), (1, 0)])

    most = wide_sum(*both_cores([here, across, right, left], False))
    most = lax.psum_scatter(most, "z", scatter_dimension=0, tiled=True)
    rest = both_cores([left_across, right_across, far_across, far], True)

    def terms(by):
        return [r[n_y * by : n_y * (by + 1)] for r in rest]

    half = n_z // 2
    up = wide_sum(*terms(half))
    for by in range(half - 1, 0, -1):
        up = wide_sum(shift(up, "z", 1), *terms(by))
    down = wide_sum(*terms(half + 1))
    for by in range(half + 2, n_z):
        down = wide_sum(shift(down, "z", -1), *terms(by))
    rest = wide_sum(shift(up, "z", 1), shift(down, "z", -1), *terms(0))

    by_place = jnp.stack(
        [
            jnp.stack([most[:, 0], most[:, 2], rest[:, 3], most[:, 3]], axis=1),
            jnp.stack([most[:, 1], rest[:, 1], rest[:, 2], rest[:, 0]], axis=1),
        ],
        axis=1,
    )
    by_place = jnp.where(y == 1, by_place[:, ::-1], by_place)
    by_place = lax.dynamic_slice_in_dim(
        jnp.concatenate([by_place, by_place], axis=2), (n_x - x) % n_x, n_x, axis=2
    )
    pieces = by_place.reshape(n_y * 2 * n_x, keep, columns)
    pieces = lax.all_to_all(pieces, ("y_hi", "y_lo", "x"), 0, 0, tiled=True)
    pieces = pieces.reshape(n_y, 2 * n_x, keep, columns)
    total = wide_sum(pieces[0], pieces[1])
    return jnp.swapaxes(total, 0, 1).reshape(keep, 2 * n_x * columns)


def solution(mesh):
    names = ("y_lo", "x", "z", "y_hi", "core")
    split = Mesh(mesh.devices.reshape(2, mesh.shape["blk"] // 2, mesh.shape["grp"] // 4, 2, 2), names)
    blk, grp = names[:2], names[2:]
    in_specs = (P(blk, None, grp), P(blk, None, grp), P(blk), P(blk, None), P(blk, grp, None))
    return jax.shard_map(
        on_device, mesh=split, in_specs=in_specs, out_specs=P(names, None), check_vma=False
    )
```
